32 devices in a mesh: tx: 2 (over y), ty: 4 (over z), gz: 4 (over x, core).
Axes of the slice: x: 2, y: 2, z: 4, core: 2. Of those that a mesh axis runs over, the one named last changes fastest.
Arguments:
- tracer_in: float32 [100, 256, 256], P('gz', 'ty', 'tx'), may hold values from -6 to 6
- coef_h: float32 [3, 256, 256], P(None, 'ty', 'tx'), may hold values from 0.05 to 0.2
- coef_v: float32 [3, 100], replicated, may hold values from 0.3 to 1
- wet_levels: int32 [256, 256], P('ty', 'tx'), may hold values from 0 to 100
- column_inv: float32 [100, 100], replicated, may hold values from -0.1 to 1
- sec_cell: int32 [2048], P(('tx', 'ty')), may hold values from 0 to 8191
- sec_gate: int32 [2048], P(('tx', 'ty')), may hold values from 0 to 63
- sec_weight: float32 [2048], P(('tx', 'ty')), may hold values from -6 to 6
Outputs:
- tracer_out: float32 [100, 256, 256], P('gz', 'ty', 'tx')
- gate_flux: float32 [64, 100], P(('tx', 'ty'), 'gz')
The draws below stay inside these ranges and needn't reach their ends.
Inputs may be any that keep to these rules, and one draw needn't show every extreme that they name: `sec_cell`: index of a cell within the tile of the slot.
All inputs are finite; a program needn't handle non-finite values.
Results may differ from the reference program's by a relative error of at most 0.00015.
Values sent between devices are 32-bit elements; how exact they have to be, the bound alone decides.
A program may use at most 64 MiB of HBM per device.

```python
import math
import jax
import jax.numpy as jnp
import numpy as np
from jax import lax

K = 100
NSUB = 3
STEPS = 2
CY = 64
CX = 128
SLOT_DEV = 256
NY = 256
NX = 256
G = 64
SLOTS = 2048
N_TY = 4


def draw_column_inv(key, part):
    key_diag, key_off = jax.random.split(key)
    diagonal = jax.random.uniform(key_diag, (K,), jnp.float32, 0.5, 0.9)
    offset = jax.random.truncated_normal(key_off, -3.0, 3.0, (K, K), jnp.float32) * (0.3 / math.sqrt(K))
    return offset + jnp.eye(K, dtype=jnp.float32) * diagonal[:, None]


def set_ends(entries, own_key, low, high):
    spot = [jax.random.randint(jax.random.fold_in(own_key, axis), (), 0, length) for axis, length in enumerate(entries.shape)]
    longest = entries.shape.index(max(entries.shape))
    beside = spot[:longest] + [(spot[longest] + 1) % entries.shape[longest]] + spot[longest + 1:]
    return entries.at[tuple(spot)].set(low).at[tuple(beside)].set(high)


def level_of(stream_key, dims, shards, least, top_value):
    gain, own = 1.0, jax.random.fold_in(stream_key, 6)
    for position, parts in shards:
        steps = jnp.exp(jax.random.uniform(jax.random.fold_in(own, position), (parts,), jnp.float32, least / len(shards), top_value / len(shards)))
        gain = gain * jnp.repeat(steps, dims[position] // parts).reshape([-1 if axis == position else 1 for axis in range(len(dims))])
    return gain


def rank_table(number_of, lean):
    portions = [(1 << 20) // math.isqrt(standing ** lean) + 1 for standing in range(1, number_of + 1)]
    scale = 1 + sum(portions) // (1 << 30)
    return np.cumsum(np.array([max(1, weight // scale) for weight in portions]))


def skewed_ids(own_key, extent, amount, slope):
    table = rank_table(amount, slope)
    ticket = jax.random.randint(jax.random.fold_in(own_key, 1), extent, 0, int(table[amount - 1]))
    rank = jnp.searchsorted(jnp.asarray(table, jnp.int32), ticket, side="right")
    return jax.random.permutation(jax.random.fold_in(own_key, 2), amount)[rank].astype(jnp.int32)


def centred(key, dims, deviation, reach, cuts=(), kind=jnp.bfloat16):
    result = deviation * jax.random.normal(key, dims, jnp.float32)
    if cuts:
        result = result * level_of(key, dims, cuts, -0.22, 0.18)
    return jnp.clip(result, -reach, reach).astype(kind)


def setup_inputs(seed: int = 0) -> dict:
    seeds = jax.random.split(jax.random.key(seed), 9)
    return {
        "tracer_in": centred(seeds[0], (K, NY, NX), 1.0, 6.0, ((0, 4), (1, 4), (2, 2)), jnp.float32),
        "coef_h": jnp.clip(0.05 + 0.15 * jax.random.uniform(seeds[1], (3, NY, NX), jnp.float32) ** level_of(seeds[1], (3, NY, NX), ((1, 4), (2, 2)), -0.2, 0.2), 0.05, 0.2),
        "coef_v": jnp.clip(jnp.exp(jax.random.uniform(seeds[2], (3, K), jnp.float32, math.log(0.3), math.log(1.0))), 0.3, 1.0),
        "wet_levels": set_ends(jax.random.randint(seeds[3], (NY, NX), 0, K + 1), jax.random.fold_in(seeds[3], 1), 0, K).astype(jnp.int32),
        "column_inv": draw_column_inv(jax.random.fold_in(seeds[8], 71), 0),
        "sec_cell": set_ends(jax.random.randint(seeds[5], (SLOTS,), 0, CY * CX), jax.random.fold_in(seeds[5], 1), 0, (CY * CX) - 1).astype(jnp.int32),
        "sec_gate": set_ends(skewed_ids(seeds[6], (SLOTS,), G, 1), jax.random.fold_in(seeds[6], 3), 0, G - 1).astype(jnp.int32),
        "sec_weight": centred(seeds[7], (SLOTS,), 1.0, 6.0, ((0, 8),), jnp.float32),
    }


def diffuse(padded, coef_h, coef_v, wet):
    centre = padded[:, 1:-1, 1:-1]
    coef_x = coef_h[0][None] * coef_v[0][:, None, None]
    coef_y = coef_h[1][None] * coef_v[1][:, None, None]
    coef_s = coef_h[2][None] * coef_v[2][:, None, None]
    along_x = padded[:, 1:-1, 2:] - 2.0 * centre + padded[:, 1:-1, :-2]
    along_y = padded[:, 2:, 1:-1] - 2.0 * centre + padded[:, :-2, 1:-1]
    cross = padded[:, 2:, 2:] - padded[:, 2:, :-2] - padded[:, :-2, 2:] + padded[:, :-2, :-2]
    return wet * (centre + coef_x * along_x + coef_y * along_y + 0.25 * coef_s * cross)


def vertical(field, column_inv, wet):
    levels = column_inv.shape[0]
    flat = field.reshape(levels, -1)
    solved = jnp.dot(column_inv.T, flat, precision=lax.Precision.HIGHEST)
    return wet * solved.reshape(field.shape)


def reference(tracer_in, coef_h, coef_v, wet_levels, column_inv, sec_cell, sec_gate, sec_weight):
    wet = (jnp.arange(K, dtype=jnp.int32)[:, None, None] < wet_levels[None]).astype(jnp.float32)
    adjoint = wet * tracer_in
    tile = jnp.arange(SLOTS, dtype=jnp.int32) // SLOT_DEV
    tile_x = tile // N_TY
    tile_y = tile % N_TY
    grid_row = tile_y * CY + sec_cell // CX
    grid_col = tile_x * CX + sec_cell % CX
    flat_index = (grid_row * NX + grid_col).astype(jnp.int32)
    gate_flux = jnp.zeros((G, K), jnp.float32)
    for step_index in range(STEPS):
        for substep in range(NSUB):
            padded = jnp.pad(adjoint, ((0, 0), (1, 1), (1, 1)))
            adjoint = diffuse(padded, coef_h, coef_v, wet)
        adjoint = vertical(adjoint, column_inv, wet)
        values = adjoint.reshape(K, NY * NX)[:, flat_index]
        weighted = (sec_weight[None, :] * values).T
        gate_flux = gate_flux + jax.ops.segment_sum(weighted, sec_gate, num_segments=G)
    return adjoint, gate_flux
```

```python
import jax
import jax.numpy as jnp
from jax import lax
from jax.sharding import PartitionSpec as P

NSUB = 3
G_DEV = 8
HI = lax.Precision.HIGHEST


def extended(block, axis, dim, width):
    count = lax.axis_size(axis)
    forward = [(i, i + 1) for i in range(count - 1)]
    backward = [(target, source) for source, target in forward]
    low = lax.ppermute(
        lax.slice_in_dim(block, block.shape[dim] - width, None, axis=dim), axis, forward
    )
    high = lax.ppermute(lax.slice_in_dim(block, 0, width, axis=dim), axis, backward)
    return jnp.concatenate([low, block, high], axis=dim)


def diffuse(padded, coef_h, coef_v, wet_levels, level_ids):
    centre = padded[:, 1:-1, 1:-1]
    coef_x = coef_h[0][None] * coef_v[0][:, None, None]
    coef_y = coef_h[1][None] * coef_v[1][:, None, None]
    coef_s = coef_h[2][None] * coef_v[2][:, None, None]
    along_x = padded[:, 1:-1, 2:] - 2.0 * centre + padded[:, 1:-1, :-2]
    along_y = padded[:, 2:, 1:-1] - 2.0 * centre + padded[:, :-2, 1:-1]
    cross = padded[:, 2:, 2:] - padded[:, 2:, :-2] - padded[:, :-2, 2:] + padded[:, :-2, :-2]
    wet = (level_ids[:, None, None] < wet_levels[None]).astype(jnp.float32)
    return wet * (centre + coef_x * along_x + coef_y * along_y + 0.25 * coef_s * cross)


def substeps(field, coef_h, coef_v, wet_levels, level_ids):
    for ring in range(1, NSUB + 1):
        inner = coef_h[:, ring:-ring, ring:-ring]
        field = diffuse(field, inner, coef_v, wet_levels[ring:-ring, ring:-ring], level_ids)
    return field


def vertical(field, column_inv, wet_levels, level_ids):
    levels = column_inv.shape[0]
    flat = field.reshape(levels, -1)
    solved = jnp.dot(column_inv.T, flat, precision=HI).reshape(field.shape)
    wet = (level_ids[:, None, None] < wet_levels[None]).astype(jnp.float32)
    return wet * solved


def per_device(tracer_in, coef_h, coef_v, wet_levels, column_inv, sec_cell, sec_gate, sec_weight):
    depth_count = lax.axis_size("gz")
    depth_index = lax.axis_index("gz")
    tiles = lax.axis_size(("tx", "ty"))
    local_levels, rows, width = tracer_in.shape
    levels = local_levels * depth_count
    col_rows = rows // depth_count
    level_ids = depth_index * local_levels + jnp.arange(local_levels, dtype=jnp.int32)
    all_ids = jnp.arange(levels, dtype=jnp.int32)
    coef_depth = lax.dynamic_slice_in_dim(coef_v, depth_index * local_levels, local_levels, 1)
    row_start = depth_index * col_rows

    gate_ids = jnp.arange(G_DEV * tiles, dtype=jnp.int32)
    gate_hot = jnp.where(gate_ids[:, None] == sec_gate[None, :], sec_weight[None, :], 0.0)
    cells = row_start * width + jnp.arange(col_rows * width, dtype=jnp.int32)
    cell_hot = (sec_cell[:, None] == cells[None, :]).astype(jnp.float32)
    gate_cells = jnp.dot(gate_hot, cell_hot, precision=HI)

    rim = 2 * NSUB
    wet_depth = (level_ids[:, None, None] < wet_levels[None]).astype(jnp.float32)
    packed = jnp.concatenate(
        [wet_depth * tracer_in, coef_h, wet_levels[None].astype(jnp.float32)], axis=0
    )
    packed = extended(extended(packed, "tx", 2, rim), "ty", 1, rim)
    field = packed[:local_levels]
    coef_h = packed[local_levels:-1]
    wet_levels = packed[-1].astype(jnp.int32)

    field = substeps(field, coef_h, coef_depth, wet_levels, level_ids)
    tall = col_rows + 2 * NSUB
    sent = jnp.stack(
        [field[:, part * col_rows : part * col_rows + tall, :] for part in range(depth_count)]
    )
    sent = sent.reshape(depth_count, local_levels, -1)
    field = lax.all_to_all(sent, "gz", split_axis=0, concat_axis=0, tiled=True)
    field = field.reshape(levels, tall, -1)
    coef_h = lax.dynamic_slice_in_dim(coef_h, row_start + NSUB, tall, 1)[:, :, NSUB:-NSUB]
    wet_levels = lax.dynamic_slice_in_dim(wet_levels, row_start + NSUB, tall, 0)[:, NSUB:-NSUB]
    field = vertical(field, column_inv, wet_levels, all_ids)
    total = field[:, NSUB:-NSUB, NSUB:-NSUB]

    field = substeps(field, coef_h, coef_v, wet_levels, all_ids)
    field = vertical(field, column_inv, wet_levels[NSUB:-NSUB, NSUB:-NSUB], all_ids)
    total = total + field
    out = lax.all_to_all(field, "gz", split_axis=0, concat_axis=1, tiled=True)

    flux = lax.dot_general(
        gate_cells, total.reshape(levels, -1), (((1,), (1,)), ((), ())), precision=HI
    )
    flux = flux.reshape(tiles, G_DEV, depth_count, local_levels).transpose(0, 2, 1, 3)
    flux = flux.reshape(tiles * depth_count, G_DEV * local_levels)
    flux = lax.all_to_all(flux, ("tx", "ty", "gz"), split_axis=0, concat_axis=0, tiled=True)
    flux = jnp.sum(flux, axis=0).reshape(G_DEV, local_levels)
    return (out, flux)


def solution(mesh):
    in_specs = (
        P("gz", "ty", "tx"),
        P(None, "ty", "tx"),
        P(),
        P("ty", "tx"),
        P(),
        P(("tx", "ty")),
        P(("tx", "ty")),
        P(("tx", "ty")),
    )
    out_specs = (P("gz", "ty", "tx"), P(("tx", "ty"), "gz"))
    return jax.shard_map(
        per_device, mesh=mesh, in_specs=in_specs, out_specs=out_specs, check_vma=False
    )
```

```python
import jax
import jax.numpy as jnp
from jax import lax
from jax.experimental import pallas as pl
from jax.experimental.pallas import tpu as pltpu
from jax.sharding import PartitionSpec as P

NSUB = 3
G_DEV = 8
HI = lax.Precision.HIGHEST


def extended(block, axis, dim, width):
    count = lax.axis_size(axis)
    forward = [(i, i + 1) for i in range(count - 1)]
    backward = [(target, source) for source, target in forward]
    low = lax.ppermute(
        lax.slice_in_dim(block, block.shape[dim] - width, None, axis=dim), axis, forward
    )
    high = lax.ppermute(lax.slice_in_dim(block, 0, width, axis=dim), axis, backward)
    return jnp.concatenate([low, block, high], axis=dim)

LANES = 128
VMEM = pl.BlockSpec(memory_space=pltpu.VMEM)
SMEM = pl.BlockSpec(memory_space=pltpu.SMEM)
OFF = 4
PARAMS = pltpu.CompilerParams(vmem_limit_bytes=48 * 1024 * 1024)


def substeps(a, wet, kx, ky, ks):
    kx, ky, ks = wet * kx, wet * ky, wet * (0.25 * ks)
    rows, lanes = a.shape
    for _ in range(NSUB):
        east, west = pltpu.roll(a, lanes - 1, 1), pltpu.roll(a, 1, 1)
        north, south = pltpu.roll(a, rows - 1, 0), pltpu.roll(a, 1, 0)
        slope = east - west
        cross = pltpu.roll(slope, rows - 1, 0) - pltpu.roll(slope, 1, 0)
        twice = 2.0 * a
        a = wet * a + kx * (east - twice + west) + ky * (north - twice + south) + ks * cross
    return a


def levels_kernel(local, parts, col_rows, base_ref, cv_ref, p_ref, out_ref, side):
    tiles = (col_rows + 8) // 8
    coefs = [p_ref.at[local + c] for c in range(3)]

    def level(l, carry):
        k = (base_ref[0] + l).astype(jnp.float32)
        wet = jnp.where(k < p_ref[local + 3], 1.0, 0.0)
        a = substeps(p_ref[l], wet, *(c[...] * cv_ref[i, l] for i, c in enumerate(coefs)))
        for part in range(parts):
            for t in range(tiles):
                row = part * col_rows + 8 * t
                out_ref[part, tiles * l + t] = a[row : row + 8, :LANES]
        side[l] = a[:, LANES:]
        return carry

    lax.fori_loop(0, local, level, 0)
    lane = lax.broadcasted_iota(jnp.int32, (8, LANES), 1)

    def pack(q, carry):
        for part in range(parts):
            acc = jnp.zeros((8, LANES), jnp.float32)
            for j in range(5):
                for t in range(tiles):
                    slot = 8 * (tiles * j + t)
                    row = part * col_rows + 8 * t
                    tile = pltpu.roll(side[5 * q + j, row : row + 8, :], slot + NSUB, 1)
                    acc = jnp.where((lane >= slot) & (lane < slot + 2 * NSUB), tile, acc)
            out_ref[part, tiles * local + q] = acc
        return carry

    lax.fori_loop(0, local // 5, pack, 0)


def split(x):
    high = x.astype(jnp.bfloat16)
    return high, (x - high.astype(jnp.float32)).astype(jnp.bfloat16)


def columns_kernel(local, parts, col_rows, cv_ref, inv_ref, c_ref, m_ref, in_ref,
                   out_ref, flux_ref, main, side, after):
    levels = local * parts
    tall = col_rows + 8
    tiles = tall // 8
    lane = lax.broadcasted_iota(jnp.int32, (8, LANES), 1)
    rim = (lane < NSUB) | (lane >= LANES - NSUB)

    def unpack(q, carry):
        for part in range(parts):
            packed = in_ref[part, tiles * local + q]
            for j in range(5):
                for t in range(tiles):
                    shift = LANES - NSUB - 8 * (tiles * j + t)
                    row = pl.multiple_of((part * local + 5 * q + j) * tall + 8 * t, 8)
                    side[pl.ds(row, 8), :] = jnp.where(rim, pltpu.roll(packed, shift, 1), 0.0)
                    main[pl.ds(row, 8), :] = in_ref[part, tiles * (5 * q + j) + t]
        return carry

    lax.fori_loop(0, local // 5, unpack, 0)
    inv_high, inv_low = split(inv_ref[...])
    ids = lax.broadcasted_iota(jnp.int32, (levels, 2 * LANES), 0).astype(jnp.float32)

    def solve(field, bounds):
        high, low = split(field)
        dot = lambda a, b: jnp.dot(a, b, preferred_element_type=jnp.float32)
        out = dot(inv_high, high) + (dot(inv_low, high) + dot(inv_high, low))
        return jnp.where(ids < bounds, out, 0.0)

    for r in range(1, tall - 1):
        at = pl.ds(r, levels, stride=tall)
        field = jnp.concatenate([main[at, :], side[at, :]], axis=1)
        field = solve(field, c_ref[3, r : r + 1, :])
        main[at, :] = field[:, :LANES]
        side[at, :] = field[:, LANES:]

    def level(k, carry):
        at = pl.ds(pl.multiple_of(k * tall, 8), tall)
        wet = jnp.where(k.astype(jnp.float32) < c_ref[3], 1.0, 0.0)
        a = jnp.concatenate([main[at, :], side[at, :]], axis=1)
        a = substeps(a, wet, *(c_ref[i] * cv_ref[i, k] for i in range(3)))
        after[at, :] = a[:, :LANES]
        return carry

    lax.fori_loop(0, levels, level, 0)
    flux = jnp.zeros(flux_ref.shape, jnp.float32)
    for r in range(0, col_rows, 2):
        ats = [pl.ds(OFF + r + i, levels, stride=tall) for i in range(2)]
        bounds = [c_ref[3, OFF + r + i : OFF + r + i + 1, :LANES] for i in range(2)]
        field = jnp.concatenate([after[at, :] for at in ats], axis=1)
        field = solve(field, jnp.concatenate(bounds, axis=1))
        for i in range(2):
            half = field[:, i * LANES : (i + 1) * LANES]
            out_ref[pl.ds(r + i, levels, stride=col_rows), :] = half
            cells = m_ref[:, (r + i) * LANES : (r + i + 1) * LANES]
            flux += lax.dot_general(
                cells, half + main[ats[i], :], (((1,), (1,)), ((), ())), precision=HI,
                preferred_element_type=jnp.float32,
            )
    flux_ref[...] = flux


def per_device(tracer_in, coef_h, coef_v, wet_levels, column_inv, sec_cell, sec_gate, sec_weight):
    depth_count = lax.axis_size("gz")
    depth_index = lax.axis_index("gz")
    tiles = lax.axis_size(("tx", "ty"))
    local_levels, rows, width = tracer_in.shape
    levels = local_levels * depth_count
    col_rows = rows // depth_count
    tall = col_rows + 8
    level_ids = depth_index * local_levels + jnp.arange(local_levels, dtype=jnp.int32)
    coef_depth = lax.dynamic_slice_in_dim(coef_v, depth_index * local_levels, local_levels, 1)
    row_start = depth_index * col_rows

    gate_ids = jnp.arange(G_DEV * tiles, dtype=jnp.int32)
    gate_hot = jnp.where(gate_ids[:, None] == sec_gate[None, :], sec_weight[None, :], 0.0)
    cells = row_start * width + jnp.arange(col_rows * width, dtype=jnp.int32)
    cell_hot = (sec_cell[:, None] == cells[None, :]).astype(jnp.float32)
    gate_cells = jnp.dot(gate_hot, cell_hot, precision=HI)

    rim = 2 * NSUB
    wet_depth = (level_ids[:, None, None] < wet_levels[None]).astype(jnp.float32)
    packed = jnp.concatenate(
        [wet_depth * tracer_in, coef_h, wet_levels[None].astype(jnp.float32)], axis=0
    )
    packed = extended(extended(packed, "tx", 2, rim), "ty", 1, rim)
    channels = packed.shape[0]
    gap = jnp.zeros((channels, packed.shape[1], 2 * LANES - packed.shape[2]), jnp.float32)
    packed = jnp.concatenate([packed[:, :, rim:], gap, packed[:, :, :rim]], axis=2)
    gap = jnp.zeros((channels, 2 * OFF + rows + 8 - packed.shape[1], 2 * LANES), jnp.float32)
    packed = jnp.concatenate([packed[:, rim - OFF :], gap, packed[:, : rim - OFF]], axis=1)

    count = local_levels * tall // 8 + local_levels // 5
    sent = pl.pallas_call(
        lambda *refs: levels_kernel(local_levels, depth_count, col_rows, *refs),
        out_shape=jax.ShapeDtypeStruct((depth_count, count, 8, LANES), jnp.float32),
        in_specs=[SMEM, SMEM, VMEM],
        out_specs=VMEM,
        scratch_shapes=[pltpu.VMEM((local_levels, packed.shape[1], LANES), jnp.float32)],
        compiler_params=PARAMS,
    )((depth_index * local_levels)[None].astype(jnp.int32), coef_depth, packed)
    got = lax.all_to_all(sent, "gz", split_axis=0, concat_axis=0, tiled=True)

    window = lax.dynamic_slice_in_dim(packed[local_levels:], row_start, tall, 1)
    field, flux = pl.pallas_call(
        lambda *refs: columns_kernel(local_levels, depth_count, col_rows, *refs),
        out_shape=(
            jax.ShapeDtypeStruct((levels * col_rows, LANES), jnp.float32),
            jax.ShapeDtypeStruct((G_DEV * tiles, levels), jnp.float32),
        ),
        in_specs=[SMEM, VMEM, VMEM, VMEM, VMEM],
        out_specs=(VMEM, VMEM),
        scratch_shapes=[pltpu.VMEM((levels * tall, LANES), jnp.float32)] * 3,
        compiler_params=PARAMS,
    )(coef_v, column_inv.T, window, gate_cells, got)
    field = field.reshape(levels, col_rows, width)
    out = lax.all_to_all(field, "gz", split_axis=0, concat_axis=1, tiled=True)
    flux = flux.reshape(tiles, G_DEV, depth_count, local_levels).transpose(0, 2, 1, 3)
    flux = flux.reshape(tiles * depth_count, G_DEV * local_levels)
    flux = lax.all_to_all(flux, ("tx", "ty", "gz"), split_axis=0, concat_axis=0, tiled=True)
    flux = jnp.sum(flux, axis=0).reshape(G_DEV, local_levels)
    return (out, flux)


def solution(mesh):
    in_specs = (
        P("gz", "ty", "tx"),
        P(None, "ty", "tx"),
        P(),
        P("ty", "tx"),
        P(),
        P(("tx", "ty")),
        P(("tx", "ty")),
        P(("tx", "ty")),
    )
    out_specs = (P("gz", "ty", "tx"), P(("tx", "ty"), "gz"))
    return jax.shard_map(
        per_device, mesh=mesh, in_specs=in_specs, out_specs=out_specs, check_vma=False
    )
```

```python
import jax
import jax.numpy as jnp
from jax import lax
from jax.experimental import pallas as pl
from jax.experimental.pallas import tpu as pltpu
from jax.sharding import PartitionSpec as P

NSUB = 3
G_DEV = 8
HI = lax.Precision.HIGHEST


def extended(block, axis, dim, width):
    count = lax.axis_size(axis)
    forward = [(i, i + 1) for i in range(count - 1)]
    backward = [(target, source) for source, target in forward]
    low = lax.ppermute(
        lax.slice_in_dim(block, block.shape[dim] - width, None, axis=dim), axis, forward
    )
    high = lax.ppermute(lax.slice_in_dim(block, 0, width, axis=dim), axis, backward)
    return jnp.concatenate([low, block, high], axis=dim)

LANES = 128
MESH = pl.DeviceIdType.MESH
VMEM = pl.BlockSpec(memory_space=pltpu.VMEM)
SMEM = pl.BlockSpec(memory_space=pltpu.SMEM)
OFF = 4
PARAMS = pltpu.CompilerParams(vmem_limit_bytes=48 * 1024 * 1024)


def remote(number):
    return pltpu.CompilerParams(
        vmem_limit_bytes=48 * 1024 * 1024, collective_id=number, has_side_effects=True
    )


def substeps(a, wet, kx, ky, ks):
    kx, ky, ks = wet * kx, wet * ky, wet * (0.25 * ks)
    rows, lanes = a.shape
    for _ in range(NSUB):
        east, west = pltpu.roll(a, lanes - 1, 1), pltpu.roll(a, 1, 1)
        north, south = pltpu.roll(a, rows - 1, 0), pltpu.roll(a, 1, 0)
        slope = east - west
        cross = pltpu.roll(slope, rows - 1, 0) - pltpu.roll(slope, 1, 0)
        twice = 2.0 * a
        a = wet * a + kx * (east - twice + west) + ky * (north - twice + south) + ks * cross
    return a


def greet(devices):
    barrier = pltpu.get_barrier_semaphore()
    for device in devices:
        pl.semaphore_signal(barrier, inc=1, device_id=device, device_id_type=MESH)
    pl.semaphore_wait(barrier, len(devices))


def send(src, dst, sems, slot, own, device):
    return pltpu.make_async_remote_copy(
        src_ref=src, dst_ref=dst, send_sem=sems[0].at[slot], recv_sem=sems[1].at[own],
        device_id=device, device_id_type=MESH,
    )


def levels_kernel(local, parts, col_rows, cv_ref, p_ref, out_ref, block, side, send_sem, recv_sem):
    tiles = (col_rows + 8) // 8
    coefs = [p_ref.at[local + c] for c in range(3)]
    me = lax.axis_index("gz")
    tx, ty = lax.axis_index("tx"), lax.axis_index("ty")
    peers = [lax.rem(me + d, parts) for d in range(1, parts)]
    lane = lax.broadcasted_iota(jnp.int32, (8, LANES), 1)
    greet([(tx, ty, peer) for peer in peers])

    def chunk(q, carry):
        def level(j, carry):
            l = 5 * q + j
            k = (me * local + l).astype(jnp.float32)
            wet = jnp.where(k < p_ref[local + 3], 1.0, 0.0)
            a = substeps(p_ref[l], wet, *(c[...] * cv_ref[i, l] for i, c in enumerate(coefs)))
            for part in range(parts):
                for t in range(tiles):
                    row = part * col_rows + 8 * t
                    block[part, q, tiles * j + t] = a[row : row + 8, :LANES]
            side[j] = a[:, LANES:]
            return carry

        lax.fori_loop(0, 5, level, 0)
        for part in range(parts):
            acc = jnp.zeros((8, LANES), jnp.float32)
            for j in range(5):
                for t in range(tiles):
                    slot = 8 * (tiles * j + t)
                    row = part * col_rows + 8 * t
                    tile = pltpu.roll(side[j, row : row + 8, :], slot + NSUB, 1)
                    acc = jnp.where((lane >= slot) & (lane < slot + 2 * NSUB), tile, acc)
            block[part, q, 5 * tiles] = acc
        for peer in peers:
            pltpu.make_async_remote_copy(
                src_ref=block.at[peer, q], dst_ref=out_ref.at[me, q],
                send_sem=send_sem.at[peer, q], recv_sem=recv_sem.at[me, q],
                device_id=(tx, ty, peer), device_id_type=MESH,
            ).start()
        out_ref[me, q] = block[me, q]
        return carry

    chunks = local // 5
    lax.fori_loop(0, chunks, chunk, 0)

    def finish(q, carry):
        for peer in peers:
            pltpu.make_async_remote_copy(
                src_ref=block.at[peer, q], dst_ref=out_ref.at[peer, q],
                send_sem=send_sem.at[peer, q], recv_sem=recv_sem.at[peer, q],
                device_id=(tx, ty, peer), device_id_type=MESH,
            ).wait()
        return carry

    lax.fori_loop(0, chunks, finish, 0)


def result_kernel(local, parts, col_rows, n_tx, n_ty, field_ref, flux_ref, out_ref, sum_ref,
                  gates, part_flux, tile_flux, *sems):
    me = lax.axis_index("gz")
    tx, ty = lax.axis_index("tx"), lax.axis_index("ty")
    tile, tiles = tx * n_ty + ty, n_tx * n_ty
    peers = [lax.rem(me + d, parts) for d in range(1, parts)]
    others = [lax.rem(tile + d, tiles) for d in range(1, tiles)]
    rows = lambda at: pl.ds(pl.multiple_of(at * col_rows, col_rows), col_rows)
    place = lambda peer: (tx, ty, peer)
    owner = lambda other: (lax.div(other, n_ty), lax.rem(other, n_ty), me)
    gate_rows = lambda at: pl.ds(pl.multiple_of(at * G_DEV, G_DEV), G_DEV)
    greet([place(p) for p in peers] + [owner(o) for o in others])

    def copies(kind, own, peer):
        levels = pl.ds(peer * local, local)
        if kind == 0:
            return send(flux_ref.at[peer], part_flux.at[own], sems[0:2], peer, own, place(peer))
        if kind == 1:
            return send(field_ref.at[levels], out_ref.at[:, rows(own), :], sems[2:4], peer, own,
                        place(peer))
        return send(gates.at[gate_rows(peer)], tile_flux.at[own], sems[4:6], peer, own, owner(peer))

    for kind in range(2):
        for peer in peers:
            copies(kind, me, peer).start()
    out_ref[:, rows(me), :] = field_ref[pl.ds(me * local, local)]
    part_flux[me] = flux_ref[me]
    for peer in peers:
        copies(0, peer, peer).wait()
    gates[...] = jnp.sum(part_flux[...], axis=0)
    for other in others:
        copies(2, tile, other).start()
    tile_flux[tile] = gates[gate_rows(tile)]
    for other in others:
        copies(2, other, other).wait()
    sum_ref[...] = jnp.sum(tile_flux[...], axis=0)
    for peer in peers:
        copies(1, peer, peer).wait()


def split(x):
    high = x.astype(jnp.bfloat16)
    return high, (x - high.astype(jnp.float32)).astype(jnp.bfloat16)


def columns_kernel(local, parts, col_rows, cv_ref, inv_ref, c_ref, m_ref, in_ref,
                   out_ref, flux_ref, main, side, after):
    levels = local * parts
    tall = col_rows + 8
    tiles = tall // 8
    lane = lax.broadcasted_iota(jnp.int32, (8, LANES), 1)
    rim = (lane < NSUB) | (lane >= LANES - NSUB)

    def unpack(q, carry):
        for part in range(parts):
            packed = in_ref[part, q, 5 * tiles]
            for j in range(5):
                for t in range(tiles):
                    shift = LANES - NSUB - 8 * (tiles * j + t)
                    row = pl.multiple_of((part * local + 5 * q + j) * tall + 8 * t, 8)
                    side[pl.ds(row, 8), :] = jnp.where(rim, pltpu.roll(packed, shift, 1), 0.0)
                    main[pl.ds(row, 8), :] = in_ref[part, q, tiles * j + t]
        return carry

    lax.fori_loop(0, local // 5, unpack, 0)
    inv_high, inv_low = split(inv_ref[...])
    padded = inv_high.shape[0]
    inv_both = jnp.concatenate([inv_high, inv_low], axis=0)
    inv_high = inv_high[:levels]
    ids = lax.broadcasted_iota(jnp.int32, (levels, 2 * LANES), 0).astype(jnp.float32)

    def solve(field, bounds):
        high, low = split(field)
        dot = lambda a, b: jnp.dot(a, b, preferred_element_type=jnp.float32)
        both = dot(inv_both, high)
        out = both[:levels] + (both[padded : padded + levels] + dot(inv_high, low))
        return jnp.where(ids < bounds, out, 0.0)

    for r in range(1, tall - 1):
        at = pl.ds(r, levels, stride=tall)
        field = jnp.concatenate([main[at, :], side[at, :]], axis=1)
        field = solve(field, c_ref[3, r : r + 1, :])
        main[at, :] = field[:, :LANES]
        side[at, :] = field[:, LANES:]

    def group(q, carry):
        for j in range(4):
            k = 4 * q + j
            at = pl.ds(pl.multiple_of(k * tall, 8), tall)
            wet = jnp.where(k.astype(jnp.float32) < c_ref[3], 1.0, 0.0)
            a = jnp.concatenate([main[at, :], side[at, :]], axis=1)
            a = substeps(a, wet, *(c_ref[i] * cv_ref[i, k] for i in range(3)))
            after[at, :] = a[:, :LANES]
        return carry

    lax.fori_loop(0, levels // 4, group, 0)
    flux = jnp.zeros(flux_ref.shape, jnp.float32)
    for r in range(0, col_rows, 2):
        ats = [pl.ds(OFF + r + i, levels, stride=tall) for i in range(2)]
        bounds = [c_ref[3, OFF + r + i : OFF + r + i + 1, :LANES] for i in range(2)]
        field = jnp.concatenate([after[at, :] for at in ats], axis=1)
        field = solve(field, jnp.concatenate(bounds, axis=1))
        for i in range(2):
            out_ref[pl.ds(r + i, levels, stride=col_rows), :] = field[:, i * LANES : (i + 1) * LANES]
        first = jnp.concatenate([main[at, :] for at in ats], axis=1)
        cells = split(m_ref[:, r * LANES : (r + 2) * LANES])
        total = split(field + first)
        for one, two in ((0, 0), (0, 1), (1, 0)):
            flux += lax.dot_general(
                cells[one], total[two], (((1,), (1,)), ((), ())),
                preferred_element_type=jnp.float32,
            )
    flux_ref[...] = flux


def per_device(tracer_in, coef_h, coef_v, wet_levels, column_inv, sec_cell, sec_gate, sec_weight):
    depth_count = lax.axis_size("gz")
    depth_index = lax.axis_index("gz")
    tiles = lax.axis_size(("tx", "ty"))
    local_levels, rows, width = tracer_in.shape
    levels = local_levels * depth_count
    col_rows = rows // depth_count
    tall = col_rows + 8
    chunks = local_levels // 5
    level_ids = depth_index * local_levels + jnp.arange(local_levels, dtype=jnp.int32)
    coef_depth = lax.dynamic_slice_in_dim(coef_v, depth_index * local_levels, local_levels, 1)
    row_start = depth_index * col_rows

    gate_ids = jnp.arange(G_DEV * tiles, dtype=jnp.int32)
    gate_hot = jnp.where(gate_ids[:, None] == sec_gate[None, :], sec_weight[None, :], 0.0)
    cells = row_start * width + jnp.arange(col_rows * width, dtype=jnp.int32)
    cell_hot = (sec_cell[:, None] == cells[None, :]).astype(jnp.float32)
    gate_cells = jnp.dot(gate_hot, cell_hot, precision=HI)

    rim = 2 * NSUB
    wet_depth = (level_ids[:, None, None] < wet_levels[None]).astype(jnp.float32)
    packed = jnp.concatenate(
        [wet_depth * tracer_in, coef_h, wet_levels[None].astype(jnp.float32)], axis=0
    )
    packed = extended(extended(packed, "tx", 2, rim), "ty", 1, rim)
    channels = packed.shape[0]
    gap = jnp.zeros((channels, packed.shape[1], 2 * LANES - packed.shape[2]), jnp.float32)
    packed = jnp.concatenate([packed[:, :, rim:], gap, packed[:, :, :rim]], axis=2)
    gap = jnp.zeros((channels, 2 * OFF + rows + 8 - packed.shape[1], 2 * LANES), jnp.float32)
    packed = jnp.concatenate([packed[:, rim - OFF :], gap, packed[:, : rim - OFF]], axis=1)

    blocks = (depth_count, chunks, 5 * tall // 8 + 1, 8, LANES)
    dma = pltpu.SemaphoreType.DMA
    got = pl.pallas_call(
        lambda *refs: levels_kernel(local_levels, depth_count, col_rows, *refs),
        out_shape=jax.ShapeDtypeStruct(blocks, jnp.float32),
        in_specs=[SMEM, VMEM],
        out_specs=VMEM,
        scratch_shapes=[
            pltpu.VMEM(blocks, jnp.float32),
            pltpu.VMEM((5, packed.shape[1], LANES), jnp.float32),
            dma((depth_count, chunks)),
            dma((depth_count, chunks)),
        ],
        compiler_params=remote(0),
    )(coef_depth, packed)

    window = lax.dynamic_slice_in_dim(packed[local_levels:], row_start, tall, 1)
    field, flux = pl.pallas_call(
        lambda *refs: columns_kernel(local_levels, depth_count, col_rows, *refs),
        out_shape=(
            jax.ShapeDtypeStruct((levels * col_rows, LANES), jnp.float32),
            jax.ShapeDtypeStruct((G_DEV * tiles, levels), jnp.float32),
        ),
        in_specs=[SMEM, VMEM, VMEM, VMEM, VMEM],
        out_specs=(VMEM, VMEM),
        scratch_shapes=[pltpu.VMEM((levels * tall, LANES), jnp.float32)] * 3,
        compiler_params=PARAMS,
    )(coef_v, jnp.pad(column_inv.T, ((0, -levels % 16), (0, 0))), window, gate_cells, got)
    field = field.reshape(levels, col_rows, width)
    flux = flux.reshape(-1, depth_count, local_levels).transpose(1, 0, 2)
    flux = jnp.pad(flux, ((0, 0), (0, 0), (0, LANES - local_levels)))
    out, flux = pl.pallas_call(
        lambda *refs: result_kernel(
            local_levels, depth_count, col_rows, lax.axis_size("tx"), lax.axis_size("ty"), *refs
        ),
        out_shape=(
            jax.ShapeDtypeStruct((local_levels, rows, width), jnp.float32),
            jax.ShapeDtypeStruct((G_DEV, LANES), jnp.float32),
        ),
        in_specs=[VMEM, VMEM],
        out_specs=(VMEM, VMEM),
        scratch_shapes=[
            pltpu.VMEM((G_DEV * tiles, LANES), jnp.float32),
            pltpu.VMEM((depth_count, G_DEV * tiles, LANES), jnp.float32),
            pltpu.VMEM((tiles, G_DEV, LANES), jnp.float32),
        ]
        + [dma((depth_count,))] * 4
        + [dma((tiles,))] * 2,
        compiler_params=remote(1),
    )(field, flux)
    flux = flux[:, :local_levels]
    return (out, flux)


def solution(mesh):
    in_specs = (
        P("gz", "ty", "tx"),
        P(None, "ty", "tx"),
        P(),
        P("ty", "tx"),
        P(),
        P(("tx", "ty")),
        P(("tx", "ty")),
        P(("tx", "ty")),
    )
    out_specs = (P("gz", "ty", "tx"), P(("tx", "ty"), "gz"))
    return jax.shard_map(
        per_device, mesh=mesh, in_specs=in_specs, out_specs=out_specs, check_vma=False
    )
```

```python
import jax
import jax.numpy as jnp
from jax import lax
from jax.experimental import pallas as pl
from jax.experimental.pallas import tpu as pltpu
from jax.sharding import PartitionSpec as P

NSUB = 3
G_DEV = 8
HI = lax.Precision.HIGHEST


LANES = 128
MESH = pl.DeviceIdType.MESH
VMEM = pl.BlockSpec(memory_space=pltpu.VMEM)
SMEM = pl.BlockSpec(memory_space=pltpu.SMEM)
OFF = 4
PARAMS = pltpu.CompilerParams(vmem_limit_bytes=48 * 1024 * 1024)


def remote(number):
    return pltpu.CompilerParams(
        vmem_limit_bytes=48 * 1024 * 1024, collective_id=number, has_side_effects=True
    )


def substeps(a, wet, kx, ky, ks):
    kx, ky, ks = wet * kx, wet * ky, wet * (0.25 * ks)
    rows, lanes = a.shape
    for _ in range(NSUB):
        east, west = pltpu.roll(a, lanes - 1, 1), pltpu.roll(a, 1, 1)
        north, south = pltpu.roll(a, rows - 1, 0), pltpu.roll(a, 1, 0)
        slope = east - west
        cross = pltpu.roll(slope, rows - 1, 0) - pltpu.roll(slope, 1, 0)
        twice = 2.0 * a
        a = wet * a + kx * (east - twice + west) + ky * (north - twice + south) + ks * cross
    return a


def greet(devices):
    barrier = pltpu.get_barrier_semaphore()
    for device in devices:
        pl.semaphore_signal(barrier, inc=1, device_id=device, device_id_type=MESH)
    pl.semaphore_wait(barrier, len(devices))


def send(src, dst, sems, slot, own, device):
    return pltpu.make_async_remote_copy(
        src_ref=src, dst_ref=dst, send_sem=sems[0].at[slot], recv_sem=sems[1].at[own],
        device_id=device, device_id_type=MESH,
    )


def exchange_rims(n_tx, n_ty, tracer_ref, coef_ref, wet_ref, p_ref, x_sent, x_got, sems):
    tx, ty, me = lax.axis_index("tx"), lax.axis_index("ty"), lax.axis_index("gz")
    local, rows, _ = tracer_ref.shape
    wide = 2 * NSUB
    pairs = p_ref.shape[0] // 2
    lane = lax.broadcasted_iota(jnp.int32, (8, LANES), 1)
    has_next = (tx < n_tx - 1, ty < n_ty - 1)
    has_prior = (tx > 0, ty > 0)

    def fill(l, carry):
        p_ref[l, :rows, :LANES] = tracer_ref[l]
        return carry

    lax.fori_loop(0, local, fill, 0)
    for c in range(3):
        p_ref[local + c, :rows, :LANES] = coef_ref[c]
    p_ref[local + 3, :rows, :LANES] = wet_ref[...].astype(jnp.float32)
    for c in range(local + 4, p_ref.shape[0]):
        p_ref[c, :rows, :LANES] = jnp.zeros((rows, LANES), jnp.float32)

    def copy(kind, way):
        step = 1 - 2 * way
        if kind == 0:
            src, dst, device = x_sent.at[way], x_got.at[way], (tx + step, ty, me)
        else:
            half = pl.ds((kind - 1) * LANES, LANES)
            src = p_ref.at[:, pl.ds((rows - 8) * (1 - way), 8), half]
            dst = p_ref.at[:, pl.ds(rows + 8 * (1 - way), 8), half]
            device = (tx, ty + step, me)
        return pltpu.make_async_remote_copy(
            src_ref=src, dst_ref=dst, send_sem=sems[0].at[kind, way],
            recv_sem=sems[1].at[kind, way], device_id=device, device_id_type=MESH,
        )

    def start(kind):
        axis = min(kind, 1)
        for way, there in enumerate((has_next[axis], has_prior[axis])):
            pl.when(there)(lambda way=way: copy(kind, way).start())

    def wait(kind):
        axis = min(kind, 1)
        for way in range(2):
            to, source = (has_next[axis], has_prior[axis])[:: 1 - 2 * way]
            pl.when(to)(lambda way=way: copy(kind, way).wait_send())
            pl.when(source)(lambda way=way: copy(kind, way).wait_recv())

    def turn(tile, shift):
        return pltpu.roll(tile, shift % LANES, 1) if shift % LANES else tile

    start(1)

    def pack(q, carry):
        east = west = jnp.zeros((8, LANES), jnp.float32)
        for j in range(2):
            for t in range(8):
                slot = 8 * (8 * j + t)
                tile = p_ref[2 * q + j, 8 * t : 8 * t + 8, :LANES]
                mask = (lane >= slot) & (lane < slot + wide)
                east = jnp.where(mask, turn(tile, slot + wide), east)
                west = jnp.where(mask, turn(tile, slot), west)
        x_sent[0, q] = east
        x_sent[1, q] = west
        return carry

    lax.fori_loop(0, pairs, pack, 0)
    start(0)

    @pl.when(jnp.logical_not(has_prior[0]))
    def _():
        x_got[0] = jnp.zeros(x_got.shape[1:], jnp.float32)

    @pl.when(jnp.logical_not(has_next[0]))
    def _():
        x_got[1] = jnp.zeros(x_got.shape[1:], jnp.float32)

    edge = jnp.zeros((p_ref.shape[0], 8, 2 * LANES), jnp.float32)

    @pl.when(jnp.logical_not(has_prior[1]))
    def _():
        p_ref[:, rows + 8 : rows + 16, :] = edge

    @pl.when(jnp.logical_not(has_next[1]))
    def _():
        p_ref[:, rows : rows + 8, :] = edge

    wait(0)

    def unpack(q, carry):
        low, high = x_got[0, q], x_got[1, q]
        for j in range(2):
            for t in range(8):
                slot = 8 * (8 * j + t)
                tile = jnp.where(lane >= LANES - wide, turn(low, -slot - wide), 0.0)
                tile = jnp.where(lane < wide, turn(high, -slot), tile)
                p_ref[2 * q + j, 8 * t : 8 * t + 8, LANES:] = tile
        return carry

    lax.fori_loop(0, pairs, unpack, 0)
    start(2)
    wait(1)
    wait(2)


def levels_kernel(local, parts, col_rows, n_tx, n_ty, cv_ref, tracer_ref, coef_ref, wet_ref,
                  out_ref, window_ref, p_ref, x_sent, x_got, turned, block, side,
                  rim_send, rim_recv, send_sem, recv_sem):
    tiles = (col_rows + 8) // 8
    coefs = [p_ref.at[local + c] for c in range(3)]
    me = lax.axis_index("gz")
    tx, ty = lax.axis_index("tx"), lax.axis_index("ty")
    peers = [lax.rem(me + d, parts) for d in range(1, parts)]
    lane = lax.broadcasted_iota(jnp.int32, (8, LANES), 1)
    around = [(lax.rem(tx + d, n_tx), ty, me) for d in (1, n_tx - 1)]
    around += [(tx, lax.rem(ty + d, n_ty), me) for d in (1, n_ty - 1)]
    greet([(tx, ty, peer) for peer in peers] + around)
    exchange_rims(
        n_tx, n_ty, tracer_ref, coef_ref, wet_ref, p_ref, x_sent, x_got, (rim_send, rim_recv)
    )

    def chunk(q, carry):
        def level(j, carry):
            l = 5 * q + j
            k = (me * local + l).astype(jnp.float32)
            wet = jnp.where(k < p_ref[local + 3], 1.0, 0.0)
            a = wet * p_ref[l]
            a = substeps(a, wet, *(c[...] * cv_ref[i, l] for i, c in enumerate(coefs)))
            a = pltpu.roll(a, OFF, 0)
            for part in range(parts):
                for t in range(tiles):
                    row = part * col_rows + 8 * t
                    block[part, q, tiles * j + t] = a[row : row + 8, :LANES]
            side[j] = a[:, LANES:]
            return carry

        lax.fori_loop(0, 5, level, 0)
        for part in range(parts):
            acc = jnp.zeros((8, LANES), jnp.float32)
            for j in range(5):
                for t in range(tiles):
                    slot = 8 * (tiles * j + t)
                    row = part * col_rows + 8 * t
                    tile = pltpu.roll(side[j, row : row + 8, :], slot + NSUB, 1)
                    acc = jnp.where((lane >= slot) & (lane < slot + 2 * NSUB), tile, acc)
            block[part, q, 5 * tiles] = acc
        for peer in peers:
            pltpu.make_async_remote_copy(
                src_ref=block.at[peer, q], dst_ref=out_ref.at[me, q],
                send_sem=send_sem.at[peer, q], recv_sem=recv_sem.at[me, q],
                device_id=(tx, ty, peer), device_id_type=MESH,
            ).start()
        out_ref[me, q] = block[me, q]
        return carry

    chunks = local // 5
    lax.fori_loop(0, chunks, chunk, 0)
    own = pl.ds(pl.multiple_of(me * col_rows, 8), col_rows + 8)
    for c in range(4):
        turned[...] = pltpu.roll(p_ref[local + c], OFF, 0)
        window_ref[c] = turned[own, :]

    def finish(q, carry):
        for peer in peers:
            pltpu.make_async_remote_copy(
                src_ref=block.at[peer, q], dst_ref=out_ref.at[peer, q],
                send_sem=send_sem.at[peer, q], recv_sem=recv_sem.at[peer, q],
                device_id=(tx, ty, peer), device_id_type=MESH,
            ).wait()
        return carry

    lax.fori_loop(0, chunks, finish, 0)


def result_kernel(local, parts, col_rows, n_tx, n_ty, field_ref, flux_ref, out_ref, sum_ref,
                  gates, part_flux, tile_flux, *sems):
    me = lax.axis_index("gz")
    tx, ty = lax.axis_index("tx"), lax.axis_index("ty")
    tile, tiles = tx * n_ty + ty, n_tx * n_ty
    peers = [lax.rem(me + d, parts) for d in range(1, parts)]
    others = [lax.rem(tile + d, tiles) for d in range(1, tiles)]
    rows = lambda at: pl.ds(pl.multiple_of(at * col_rows, col_rows), col_rows)
    place = lambda peer: (tx, ty, peer)
    owner = lambda other: (lax.div(other, n_ty), lax.rem(other, n_ty), me)
    gate_rows = lambda at: pl.ds(pl.multiple_of(at * G_DEV, G_DEV), G_DEV)
    greet([place(p) for p in peers] + [owner(o) for o in others])

    def copies(kind, own, peer):
        levels = pl.ds(peer * local, local)
        if kind == 0:
            return send(flux_ref.at[peer], part_flux.at[own], sems[0:2], peer, own, place(peer))
        if kind == 1:
            return send(field_ref.at[levels], out_ref.at[:, rows(own), :], sems[2:4], peer, own,
                        place(peer))
        return send(gates.at[gate_rows(peer)], tile_flux.at[own], sems[4:6], peer, own, owner(peer))

    for kind in range(2):
        for peer in peers:
            copies(kind, me, peer).start()
    out_ref[:, rows(me), :] = field_ref[pl.ds(me * local, local)]
    part_flux[me] = flux_ref[me]
    for peer in peers:
        copies(0, peer, peer).wait()
    gates[...] = jnp.sum(part_flux[...], axis=0)
    for other in others:
        copies(2, tile, other).start()
    tile_flux[tile] = gates[gate_rows(tile)]
    for other in others:
        copies(2, other, other).wait()
    sum_ref[...] = jnp.sum(tile_flux[...], axis=0)
    for peer in peers:
        copies(1, peer, peer).wait()


def split(x):
    high = x.astype(jnp.bfloat16)
    return high, (x - high.astype(jnp.float32)).astype(jnp.bfloat16)


def columns_kernel(local, parts, col_rows, cv_ref, inv_ref, c_ref, m_ref, in_ref,
                   out_ref, flux_ref, main, side, after):
    levels = local * parts
    tall = col_rows + 8
    tiles = tall // 8
    lane = lax.broadcasted_iota(jnp.int32, (8, LANES), 1)
    rim = (lane < NSUB) | (lane >= LANES - NSUB)

    def unpack(q, carry):
        for part in range(parts):
            packed = in_ref[part, q, 5 * tiles]
            for j in range(5):
                for t in range(tiles):
                    shift = LANES - NSUB - 8 * (tiles * j + t)
                    row = pl.multiple_of((part * local + 5 * q + j) * tall + 8 * t, 8)
                    side[pl.ds(row, 8), :] = jnp.where(rim, pltpu.roll(packed, shift, 1), 0.0)
                    main[pl.ds(row, 8), :] = in_ref[part, q, tiles * j + t]
        return carry

    lax.fori_loop(0, local // 5, unpack, 0)
    inv_high, inv_low = split(inv_ref[...])
    padded = inv_high.shape[0]
    inv_both = jnp.concatenate([inv_high, inv_low], axis=0)
    inv_high = inv_high[:levels]
    ids = lax.broadcasted_iota(jnp.int32, (levels, 2 * LANES), 0).astype(jnp.float32)

    def solve(field, bounds):
        high, low = split(field)
        dot = lambda a, b: jnp.dot(a, b, preferred_element_type=jnp.float32)
        both = dot(inv_both, high)
        out = both[:levels] + (both[padded : padded + levels] + dot(inv_high, low))
        return jnp.where(ids < bounds, out, 0.0)

    for r in range(1, tall - 1):
        at = pl.ds(r, levels, stride=tall)
        field = jnp.concatenate([main[at, :], side[at, :]], axis=1)
        field = solve(field, c_ref[3, r : r + 1, :])
        main[at, :] = field[:, :LANES]
        side[at, :] = field[:, LANES:]

    def group(q, carry):
        for j in range(4):
            k = 4 * q + j
            at = pl.ds(pl.multiple_of(k * tall, 8), tall)
            wet = jnp.where(k.astype(jnp.float32) < c_ref[3], 1.0, 0.0)
            a = jnp.concatenate([main[at, :], side[at, :]], axis=1)
            a = substeps(a, wet, *(c_ref[i] * cv_ref[i, k] for i in range(3)))
            after[at, :] = a[:, :LANES]
        return carry

    lax.fori_loop(0, levels // 4, group, 0)
    flux = jnp.zeros(flux_ref.shape, jnp.float32)
    for r in range(0, col_rows, 2):
        ats = [pl.ds(OFF + r + i, levels, stride=tall) for i in range(2)]
        bounds = [c_ref[3, OFF + r + i : OFF + r + i + 1, :LANES] for i in range(2)]
        field = jnp.concatenate([after[at, :] for at in ats], axis=1)
        field = solve(field, jnp.concatenate(bounds, axis=1))
        for i in range(2):
            out_ref[pl.ds(r + i, levels, stride=col_rows), :] = field[:, i * LANES : (i + 1) * LANES]
        first = jnp.concatenate([main[at, :] for at in ats], axis=1)
        cells = split(m_ref[:, r * LANES : (r + 2) * LANES])
        total = split(field + first)
        for one, two in ((0, 0), (0, 1), (1, 0)):
            flux += lax.dot_general(
                cells[one], total[two], (((1,), (1,)), ((), ())),
                preferred_element_type=jnp.float32,
            )
    flux_ref[...] = flux


def per_device(tracer_in, coef_h, coef_v, wet_levels, column_inv, sec_cell, sec_gate, sec_weight):
    depth_count = lax.axis_size("gz")
    depth_index = lax.axis_index("gz")
    tiles = lax.axis_size(("tx", "ty"))
    local_levels, rows, width = tracer_in.shape
    levels = local_levels * depth_count
    col_rows = rows // depth_count
    tall = col_rows + 8
    chunks = local_levels // 5
    coef_depth = lax.dynamic_slice_in_dim(coef_v, depth_index * local_levels, local_levels, 1)
    row_start = depth_index * col_rows

    gate_ids = jnp.arange(G_DEV * tiles, dtype=jnp.int32)
    gate_hot = jnp.where(gate_ids[:, None] == sec_gate[None, :], sec_weight[None, :], 0.0)
    cells = row_start * width + jnp.arange(col_rows * width, dtype=jnp.int32)
    cell_hot = (sec_cell[:, None] == cells[None, :]).astype(jnp.float32)
    gate_cells = jnp.dot(gate_hot, cell_hot, precision=HI)

    channels = local_levels + 4 + (local_levels + 4) % 2
    blocks = (depth_count, chunks, 5 * tall // 8 + 1, 8, LANES)
    dma = pltpu.SemaphoreType.DMA
    got, window = pl.pallas_call(
        lambda *refs: levels_kernel(
            local_levels, depth_count, col_rows, lax.axis_size("tx"), lax.axis_size("ty"), *refs
        ),
        out_shape=(
            jax.ShapeDtypeStruct(blocks, jnp.float32),
            jax.ShapeDtypeStruct((4, tall, 2 * LANES), jnp.float32),
        ),
        in_specs=[SMEM, VMEM, VMEM, VMEM],
        out_specs=(VMEM, VMEM),
        scratch_shapes=[
            pltpu.VMEM((channels, rows + 16, 2 * LANES), jnp.float32),
            pltpu.VMEM((2, channels // 2, 8, LANES), jnp.float32),
            pltpu.VMEM((2, channels // 2, 8, LANES), jnp.float32),
            pltpu.VMEM((rows + 16, 2 * LANES), jnp.float32),
            pltpu.VMEM(blocks, jnp.float32),
            pltpu.VMEM((5, rows + 16, LANES), jnp.float32),
            dma((3, 2)),
            dma((3, 2)),
            dma((depth_count, chunks)),
            dma((depth_count, chunks)),
        ],
        compiler_params=remote(0),
    )(coef_depth, tracer_in, coef_h, wet_levels)

    field, flux = pl.pallas_call(
        lambda *refs: columns_kernel(local_levels, depth_count, col_rows, *refs),
        out_shape=(
            jax.ShapeDtypeStruct((levels * col_rows, LANES), jnp.float32),
            jax.ShapeDtypeStruct((G_DEV * tiles, levels), jnp.float32),
        ),
        in_specs=[SMEM, VMEM, VMEM, VMEM, VMEM],
        out_specs=(VMEM, VMEM),
        scratch_shapes=[pltpu.VMEM((levels * tall, LANES), jnp.float32)] * 3,
        compiler_params=PARAMS,
    )(coef_v, jnp.pad(column_inv.T, ((0, -levels % 16), (0, 0))), window, gate_cells, got)
    field = field.reshape(levels, col_rows, width)
    flux = flux.reshape(-1, depth_count, local_levels).transpose(1, 0, 2)
    flux = jnp.pad(flux, ((0, 0), (0, 0), (0, LANES - local_levels)))
    out, flux = pl.pallas_call(
        lambda *refs: result_kernel(
            local_levels, depth_count, col_rows, lax.axis_size("tx"), lax.axis_size("ty"), *refs
        ),
        out_shape=(
            jax.ShapeDtypeStruct((local_levels, rows, width), jnp.float32),
            jax.ShapeDtypeStruct((G_DEV, LANES), jnp.float32),
        ),
        in_specs=[VMEM, VMEM],
        out_specs=(VMEM, VMEM),
        scratch_shapes=[
            pltpu.VMEM((G_DEV * tiles, LANES), jnp.float32),
            pltpu.VMEM((depth_count, G_DEV * tiles, LANES), jnp.float32),
            pltpu.VMEM((tiles, G_DEV, LANES), jnp.float32),
        ]
        + [dma((depth_count,))] * 4
        + [dma((tiles,))] * 2,
        compiler_params=remote(1),
    )(field, flux)
    flux = flux[:, :local_levels]
    return (out, flux)


def solution(mesh):
    in_specs = (
        P("gz", "ty", "tx"),
        P(None, "ty", "tx"),
        P(),
        P("ty", "tx"),
        P(),
        P(("tx", "ty")),
        P(("tx", "ty")),
        P(("tx", "ty")),
    )
    out_specs = (P("gz", "ty", "tx"), P(("tx", "ty"), "gz"))
    return jax.shard_map(
        per_device, mesh=mesh, in_specs=in_specs, out_specs=out_specs, check_vma=False
    )
```

```python
import jax
import jax.numpy as jnp
from jax import lax
from jax.experimental import pallas as pl
from jax.experimental.pallas import tpu as pltpu
from jax.sharding import PartitionSpec as P

NSUB = 3
G_DEV = 8
HI = lax.Precision.HIGHEST


LANES = 128
MESH = pl.DeviceIdType.MESH
VMEM = pl.BlockSpec(memory_space=pltpu.VMEM)
SMEM = pl.BlockSpec(memory_space=pltpu.SMEM)
OFF = 4

def remote(number):
    return pltpu.CompilerParams(
        vmem_limit_bytes=48 * 1024 * 1024, collective_id=number, has_side_effects=True
    )


def substeps(a, wet, kx, ky, ks):
    kx, ky, ks = wet * kx, wet * ky, wet * (0.25 * ks)
    rows, lanes = a.shape
    for _ in range(NSUB):
        east, west = pltpu.roll(a, lanes - 1, 1), pltpu.roll(a, 1, 1)
        north, south = pltpu.roll(a, rows - 1, 0), pltpu.roll(a, 1, 0)
        slope = east - west
        cross = pltpu.roll(slope, rows - 1, 0) - pltpu.roll(slope, 1, 0)
        twice = 2.0 * a
        a = wet * a + kx * (east - twice + west) + ky * (north - twice + south) + ks * cross
    return a


def greet(devices):
    barrier = pltpu.get_barrier_semaphore()
    for device in devices:
        pl.semaphore_signal(barrier, inc=1, device_id=device, device_id_type=MESH)
    pl.semaphore_wait(barrier, len(devices))


def send(src, dst, sems, slot, own, device):
    return pltpu.make_async_remote_copy(
        src_ref=src, dst_ref=dst, send_sem=sems[0].at[slot], recv_sem=sems[1].at[own],
        device_id=device, device_id_type=MESH,
    )


def exchange_rims(n_tx, n_ty, tracer_ref, coef_ref, wet_ref, p_ref, x_sent, x_got, sems):
    tx, ty, me = lax.axis_index("tx"), lax.axis_index("ty"), lax.axis_index("gz")
    local, rows, _ = tracer_ref.shape
    wide = 2 * NSUB
    pairs = p_ref.shape[0] // 2
    lane = lax.broadcasted_iota(jnp.int32, (8, LANES), 1)
    has_next = (tx < n_tx - 1, ty < n_ty - 1)
    has_prior = (tx > 0, ty > 0)

    def fill(l, carry):
        p_ref[l, :rows, :LANES] = tracer_ref[l]
        return carry

    lax.fori_loop(0, local, fill, 0)
    for c in range(3):
        p_ref[local + c, :rows, :LANES] = coef_ref[c]
    p_ref[local + 3, :rows, :LANES] = wet_ref[...].astype(jnp.float32)
    for c in range(local + 4, p_ref.shape[0]):
        p_ref[c, :rows, :LANES] = jnp.zeros((rows, LANES), jnp.float32)

    def copy(kind, way):
        step = 1 - 2 * way
        if kind == 0:
            src, dst, device = x_sent.at[way], x_got.at[way], (tx + step, ty, me)
        else:
            half = pl.ds((kind - 1) * LANES, LANES)
            src = p_ref.at[:, pl.ds((rows - 8) * (1 - way), 8), half]
            dst = p_ref.at[:, pl.ds(rows + 8 * (1 - way), 8), half]
            device = (tx, ty + step, me)
        return pltpu.make_async_remote_copy(
            src_ref=src, dst_ref=dst, send_sem=sems[0].at[kind, way],
            recv_sem=sems[1].at[kind, way], device_id=device, device_id_type=MESH,
        )

    def start(kind):
        axis = min(kind, 1)
        for way, there in enumerate((has_next[axis], has_prior[axis])):
            pl.when(there)(lambda way=way: copy(kind, way).start())

    def wait(kind):
        axis = min(kind, 1)
        for way in range(2):
            to, source = (has_next[axis], has_prior[axis])[:: 1 - 2 * way]
            pl.when(to)(lambda way=way: copy(kind, way).wait_send())
            pl.when(source)(lambda way=way: copy(kind, way).wait_recv())

    def turn(tile, shift):
        return pltpu.roll(tile, shift % LANES, 1) if shift % LANES else tile

    start(1)

    def pack(q, carry):
        east = west = jnp.zeros((8, LANES), jnp.float32)
        for j in range(2):
            for t in range(8):
                slot = 8 * (8 * j + t)
                tile = p_ref[2 * q + j, 8 * t : 8 * t + 8, :LANES]
                mask = (lane >= slot) & (lane < slot + wide)
                east = jnp.where(mask, turn(tile, slot + wide), east)
                west = jnp.where(mask, turn(tile, slot), west)
        x_sent[0, q] = east
        x_sent[1, q] = west
        return carry

    lax.fori_loop(0, pairs, pack, 0)
    start(0)

    @pl.when(jnp.logical_not(has_prior[0]))
    def _():
        x_got[0] = jnp.zeros(x_got.shape[1:], jnp.float32)

    @pl.when(jnp.logical_not(has_next[0]))
    def _():
        x_got[1] = jnp.zeros(x_got.shape[1:], jnp.float32)

    edge = jnp.zeros((p_ref.shape[0], 8, 2 * LANES), jnp.float32)

    @pl.when(jnp.logical_not(has_prior[1]))
    def _():
        p_ref[:, rows + 8 : rows + 16, :] = edge

    @pl.when(jnp.logical_not(has_next[1]))
    def _():
        p_ref[:, rows : rows + 8, :] = edge

    wait(0)

    def unpack(q, carry):
        low, high = x_got[0, q], x_got[1, q]
        for j in range(2):
            for t in range(8):
                slot = 8 * (8 * j + t)
                tile = jnp.where(lane >= LANES - wide, turn(low, -slot - wide), 0.0)
                tile = jnp.where(lane < wide, turn(high, -slot), tile)
                p_ref[2 * q + j, 8 * t : 8 * t + 8, LANES:] = tile
        return carry

    lax.fori_loop(0, pairs, unpack, 0)
    start(2)
    wait(1)
    wait(2)


def levels_kernel(local, parts, col_rows, n_tx, n_ty, cv_ref, tracer_ref, coef_ref, wet_ref,
                  out_ref, window_ref, p_ref, x_sent, x_got, turned, block, side,
                  rim_send, rim_recv, send_sem, recv_sem):
    tiles = (col_rows + 8) // 8
    coefs = [p_ref.at[local + c] for c in range(3)]
    me = lax.axis_index("gz")
    tx, ty = lax.axis_index("tx"), lax.axis_index("ty")
    peers = [lax.rem(me + d, parts) for d in range(1, parts)]
    lane = lax.broadcasted_iota(jnp.int32, (8, LANES), 1)
    around = [(lax.rem(tx + d, n_tx), ty, me) for d in (1, n_tx - 1)]
    around += [(tx, lax.rem(ty + d, n_ty), me) for d in (1, n_ty - 1)]
    greet([(tx, ty, peer) for peer in peers] + around)
    exchange_rims(
        n_tx, n_ty, tracer_ref, coef_ref, wet_ref, p_ref, x_sent, x_got, (rim_send, rim_recv)
    )

    def chunk(q, carry):
        def level(j, carry):
            l = 5 * q + j
            k = (me * local + l).astype(jnp.float32)
            wet = jnp.where(k < p_ref[local + 3], 1.0, 0.0)
            a = wet * p_ref[l]
            a = substeps(a, wet, *(c[...] * cv_ref[i, l] for i, c in enumerate(coefs)))
            a = pltpu.roll(a, OFF, 0)
            for part in range(parts):
                for t in range(tiles):
                    row = part * col_rows + 8 * t
                    block[part, q, tiles * j + t] = a[row : row + 8, :LANES]
            side[j] = a[:, LANES:]
            return carry

        lax.fori_loop(0, 5, level, 0)
        for part in range(parts):
            acc = jnp.zeros((8, LANES), jnp.float32)
            for j in range(5):
                for t in range(tiles):
                    slot = 8 * (tiles * j + t)
                    row = part * col_rows + 8 * t
                    tile = pltpu.roll(side[j, row : row + 8, :], slot + NSUB, 1)
                    acc = jnp.where((lane >= slot) & (lane < slot + 2 * NSUB), tile, acc)
            block[part, q, 5 * tiles] = acc
        for peer in peers:
            pltpu.make_async_remote_copy(
                src_ref=block.at[peer, q], dst_ref=out_ref.at[me, q],
                send_sem=send_sem.at[peer, q], recv_sem=recv_sem.at[me, q],
                device_id=(tx, ty, peer), device_id_type=MESH,
            ).start()
        out_ref[me, q] = block[me, q]
        return carry

    chunks = local // 5
    lax.fori_loop(0, chunks, chunk, 0)
    own = pl.ds(pl.multiple_of(me * col_rows, 8), col_rows + 8)
    for c in range(4):
        turned[...] = pltpu.roll(p_ref[local + c], OFF, 0)
        window_ref[c] = turned[own, :]

    def finish(q, carry):
        for peer in peers:
            pltpu.make_async_remote_copy(
                src_ref=block.at[peer, q], dst_ref=out_ref.at[peer, q],
                send_sem=send_sem.at[peer, q], recv_sem=recv_sem.at[peer, q],
                device_id=(tx, ty, peer), device_id_type=MESH,
            ).wait()
        return carry

    lax.fori_loop(0, chunks, finish, 0)


def split(x):
    high = x.astype(jnp.bfloat16)
    return high, (x - high.astype(jnp.float32)).astype(jnp.bfloat16)


def columns_kernel(local, parts, col_rows, n_tx, n_ty, cv_ref, inv_ref, c_ref, m_ref, in_ref,
                   out_ref, sum_ref, main, side, after, field_ref, got_ref, whole_flux, flux_ref,
                   gates, part_flux, tile_flux, *sems):
    levels = local * parts
    me = lax.axis_index("gz")
    tx, ty = lax.axis_index("tx"), lax.axis_index("ty")
    tile, count = tx * n_ty + ty, n_tx * n_ty
    peers = [lax.rem(me + d, parts) for d in range(1, parts)]
    others = [lax.rem(tile + d, count) for d in range(1, count)]
    place = lambda peer: (tx, ty, peer)
    owner = lambda other: (lax.div(other, n_ty), lax.rem(other, n_ty), me)
    gate_rows = lambda at: pl.ds(pl.multiple_of(at * G_DEV, G_DEV), G_DEV)
    run = 8 * local
    span = lambda half, at: pl.ds(pl.multiple_of((half * parts + at) * run, 8), run)
    greet([place(p) for p in peers] + [owner(o) for o in others])

    def copies(kind, own, peer):
        if kind == 2:
            return send(flux_ref.at[peer], part_flux.at[own], sems[4:6], peer, own, place(peer))
        if kind == 3:
            return send(gates.at[gate_rows(peer)], tile_flux.at[own], sems[6:8], peer, own,
                        owner(peer))
        return send(field_ref.at[span(kind, peer)], got_ref.at[span(kind, own)],
                    sems[2 * kind : 2 * kind + 2], peer, own, place(peer))

    tall = col_rows + 8
    tiles = tall // 8
    lane = lax.broadcasted_iota(jnp.int32, (8, LANES), 1)
    rim = (lane < NSUB) | (lane >= LANES - NSUB)

    def unpack(q, carry):
        for part in range(parts):
            packed = in_ref[part, q, 5 * tiles]
            for j in range(5):
                for t in range(tiles):
                    shift = LANES - NSUB - 8 * (tiles * j + t)
                    row = pl.multiple_of((part * local + 5 * q + j) * tall + 8 * t, 8)
                    side[pl.ds(row, 8), :] = jnp.where(rim, pltpu.roll(packed, shift, 1), 0.0)
                    main[pl.ds(row, 8), :] = in_ref[part, q, tiles * j + t]
        return carry

    lax.fori_loop(0, local // 5, unpack, 0)
    inv_high, inv_low = split(inv_ref[...])
    padded = inv_high.shape[0]
    inv_both = jnp.concatenate([inv_high, inv_low], axis=0)
    inv_high = inv_high[:levels]
    ids = lax.broadcasted_iota(jnp.int32, (levels, 2 * LANES), 0).astype(jnp.float32)

    def solve(field, bounds):
        high, low = split(field)
        dot = lambda a, b: jnp.dot(a, b, preferred_element_type=jnp.float32)
        both = dot(inv_both, high)
        out = both[:levels] + (both[padded : padded + levels] + dot(inv_high, low))
        return jnp.where(ids < bounds, out, 0.0)

    for r in range(1, tall - 1):
        at = pl.ds(r, levels, stride=tall)
        field = jnp.concatenate([main[at, :], side[at, :]], axis=1)
        field = solve(field, c_ref[3, r : r + 1, :])
        main[at, :] = field[:, :LANES]
        side[at, :] = field[:, LANES:]

    def group(q, carry):
        for j in range(4):
            k = 4 * q + j
            at = pl.ds(pl.multiple_of(k * tall, 8), tall)
            wet = jnp.where(k.astype(jnp.float32) < c_ref[3], 1.0, 0.0)
            a = jnp.concatenate([main[at, :], side[at, :]], axis=1)
            a = substeps(a, wet, *(c_ref[i] * cv_ref[i, k] for i in range(3)))
            after[at, :] = a[:, :LANES]
        return carry

    lax.fori_loop(0, levels // 4, group, 0)
    pair = lambda ref, r: jnp.concatenate(
        [ref[pl.ds(OFF + r + i, levels, stride=tall), :] for i in range(2)], axis=1
    )
    slot = lambda r: pl.ds((r // 8) * levels * 8 + r % 8, levels, stride=8)
    for r in range(0, col_rows, 2):
        bounds = [c_ref[3, OFF + r + i : OFF + r + i + 1, :LANES] for i in range(2)]
        field = solve(pair(after, r), jnp.concatenate(bounds, axis=1))
        for i in range(2):
            field_ref[slot(r + i), :] = field[:, i * LANES : (i + 1) * LANES]
        if r == 6:
            for peer in peers:
                copies(0, me, peer).start()
    flux = jnp.zeros((whole_flux.shape[0], levels), jnp.float32)
    for r in range(0, col_rows, 2):
        second = jnp.concatenate([field_ref[slot(r + i), :] for i in range(2)], axis=1)
        cells = split(m_ref[:, r * LANES : (r + 2) * LANES])
        total = split(second + pair(main, r))
        for one, two in ((0, 0), (0, 1), (1, 0)):
            flux += lax.dot_general(
                cells[one], total[two], (((1,), (1,)), ((), ())),
                preferred_element_type=jnp.float32,
            )
    whole_flux[...] = jnp.zeros(whole_flux.shape, jnp.float32)
    whole_flux[:, :levels] = flux
    for part in range(parts):
        shift = (LANES - part * local) % LANES
        shifted = whole_flux[...]
        flux_ref[part] = pltpu.roll(shifted, shift, 1) if shift else shifted
    for kind in (2, 1):
        for peer in peers:
            copies(kind, me, peer).start()
    part_flux[me] = flux_ref[me]
    for peer in peers:
        copies(2, peer, peer).wait()
    gates[...] = jnp.sum(part_flux[...], axis=0)
    for other in others:
        copies(3, tile, other).start()
    tile_flux[tile] = gates[gate_rows(tile)]
    for half in range(2):
        got_ref[span(half, me), :] = field_ref[span(half, me), :]
        for peer in peers:
            copies(half, peer, peer).wait()

    def place_level(l, carry):
        for part in range(parts):
            for half in range(2):
                row = pl.multiple_of((half * parts + part) * run + 8 * l, 8)
                start = part * col_rows + 8 * half
                out_ref[l, start : start + 8, :] = got_ref[pl.ds(row, 8), :]
        return carry

    lax.fori_loop(0, local, place_level, 0)
    for other in others:
        copies(3, other, other).wait()
    sum_ref[...] = jnp.sum(tile_flux[...], axis=0)


def per_device(tracer_in, coef_h, coef_v, wet_levels, column_inv, sec_cell, sec_gate, sec_weight):
    depth_count = lax.axis_size("gz")
    depth_index = lax.axis_index("gz")
    tiles = lax.axis_size(("tx", "ty"))
    local_levels, rows, width = tracer_in.shape
    levels = local_levels * depth_count
    col_rows = rows // depth_count
    tall = col_rows + 8
    chunks = local_levels // 5
    coef_depth = lax.dynamic_slice_in_dim(coef_v, depth_index * local_levels, local_levels, 1)
    row_start = depth_index * col_rows

    gate_ids = jnp.arange(G_DEV * tiles, dtype=jnp.int32)
    gate_hot = jnp.where(gate_ids[:, None] == sec_gate[None, :], sec_weight[None, :], 0.0)
    cells = row_start * width + jnp.arange(col_rows * width, dtype=jnp.int32)
    cell_hot = (sec_cell[:, None] == cells[None, :]).astype(jnp.float32)
    gate_cells = jnp.dot(gate_hot, cell_hot, precision=HI)

    channels = local_levels + 4 + (local_levels + 4) % 2
    blocks = (depth_count, chunks, 5 * tall // 8 + 1, 8, LANES)
    dma = pltpu.SemaphoreType.DMA
    got, window = pl.pallas_call(
        lambda *refs: levels_kernel(
            local_levels, depth_count, col_rows, lax.axis_size("tx"), lax.axis_size("ty"), *refs
        ),
        out_shape=(
            jax.ShapeDtypeStruct(blocks, jnp.float32),
            jax.ShapeDtypeStruct((4, tall, 2 * LANES), jnp.float32),
        ),
        in_specs=[SMEM, VMEM, VMEM, VMEM],
        out_specs=(VMEM, VMEM),
        scratch_shapes=[
            pltpu.VMEM((channels, rows + 16, 2 * LANES), jnp.float32),
            pltpu.VMEM((2, channels // 2, 8, LANES), jnp.float32),
            pltpu.VMEM((2, channels // 2, 8, LANES), jnp.float32),
            pltpu.VMEM((rows + 16, 2 * LANES), jnp.float32),
            pltpu.VMEM(blocks, jnp.float32),
            pltpu.VMEM((5, rows + 16, LANES), jnp.float32),
            dma((3, 2)),
            dma((3, 2)),
            dma((depth_count, chunks)),
            dma((depth_count, chunks)),
        ],
        compiler_params=remote(0),
    )(coef_depth, tracer_in, coef_h, wet_levels)

    gates = G_DEV * tiles
    out, flux = pl.pallas_call(
        lambda *refs: columns_kernel(
            local_levels, depth_count, col_rows, lax.axis_size("tx"), lax.axis_size("ty"), *refs
        ),
        out_shape=(
            jax.ShapeDtypeStruct((local_levels, rows, width), jnp.float32),
            jax.ShapeDtypeStruct((G_DEV, LANES), jnp.float32),
        ),
        in_specs=[SMEM, VMEM, VMEM, VMEM, VMEM],
        out_specs=(VMEM, VMEM),
        scratch_shapes=[pltpu.VMEM((levels * tall, LANES), jnp.float32)] * 3
        + [pltpu.VMEM((levels * col_rows, LANES), jnp.float32)] * 2
        + [
            pltpu.VMEM((gates, LANES), jnp.float32),
            pltpu.VMEM((depth_count, gates, LANES), jnp.float32),
            pltpu.VMEM((gates, LANES), jnp.float32),
            pltpu.VMEM((depth_count, gates, LANES), jnp.float32),
            pltpu.VMEM((tiles, G_DEV, LANES), jnp.float32),
        ]
        + [dma((depth_count,))] * 6
        + [dma((tiles,))] * 2,
        compiler_params=remote(1),
    )(coef_v, jnp.pad(column_inv.T, ((0, -levels % 16), (0, 0))), window, gate_cells, got)
    flux = flux[:, :local_levels]
    return (out, flux)


def solution(mesh):
    in_specs = (
        P("gz", "ty", "tx"),
        P(None, "ty", "tx"),
        P(),
        P("ty", "tx"),
        P(),
        P(("tx", "ty")),
        P(("tx", "ty")),
        P(("tx", "ty")),
    )
    out_specs = (P("gz", "ty", "tx"), P(("tx", "ty"), "gz"))
    return jax.shard_map(
        per_device, mesh=mesh, in_specs=in_specs, out_specs=out_specs, check_vma=False
    )
```

```python
import jax
import jax.numpy as jnp
from jax import lax
from jax.experimental import pallas as pl
from jax.experimental.pallas import tpu as pltpu
from jax.sharding import PartitionSpec as P

NSUB = 3
G_DEV = 8
HI = lax.Precision.HIGHEST


LANES = 128
MESH = pl.DeviceIdType.MESH
VMEM = pl.BlockSpec(memory_space=pltpu.VMEM)
SMEM = pl.BlockSpec(memory_space=pltpu.SMEM)
OFF = 4

def remote(number):
    return pltpu.CompilerParams(
        vmem_limit_bytes=48 * 1024 * 1024, collective_id=number, has_side_effects=True
    )


def substeps(a, wet, kx, ky, ks):
    kx, ky, ks = wet * kx, wet * ky, wet * (0.25 * ks)
    rows, lanes = a.shape
    for _ in range(NSUB):
        east, west = pltpu.roll(a, lanes - 1, 1), pltpu.roll(a, 1, 1)
        north, south = pltpu.roll(a, rows - 1, 0), pltpu.roll(a, 1, 0)
        slope = east - west
        cross = pltpu.roll(slope, rows - 1, 0) - pltpu.roll(slope, 1, 0)
        twice = 2.0 * a
        a = wet * a + kx * (east - twice + west) + ky * (north - twice + south) + ks * cross
    return a


def greet(devices):
    barrier = pltpu.get_barrier_semaphore()
    for device in devices:
        pl.semaphore_signal(barrier, inc=1, device_id=device, device_id_type=MESH)
    pl.semaphore_wait(barrier, len(devices))


def send(src, dst, sems, slot, own, device):
    return pltpu.make_async_remote_copy(
        src_ref=src, dst_ref=dst, send_sem=sems[0].at[slot], recv_sem=sems[1].at[own],
        device_id=device, device_id_type=MESH,
    )


def exchange_rims(n_tx, n_ty, tracer_ref, coef_ref, wet_ref, p_ref, x_sent, x_got, sems):
    tx, ty, me = lax.axis_index("tx"), lax.axis_index("ty"), lax.axis_index("gz")
    local, rows, _ = tracer_ref.shape
    wide = 2 * NSUB
    pairs = p_ref.shape[0] // 2
    lane = lax.broadcasted_iota(jnp.int32, (8, LANES), 1)
    has_next = (tx < n_tx - 1, ty < n_ty - 1)
    has_prior = (tx > 0, ty > 0)

    def fill(l, carry):
        p_ref[l, :rows, :LANES] = tracer_ref[l]
        return carry

    lax.fori_loop(0, local, fill, 0, unroll=5)
    for c in range(3):
        p_ref[local + c, :rows, :LANES] = coef_ref[c]
    p_ref[local + 3, :rows, :LANES] = wet_ref[...].astype(jnp.float32)
    for c in range(local + 4, p_ref.shape[0]):
        p_ref[c, :rows, :LANES] = jnp.zeros((rows, LANES), jnp.float32)

    def copy(kind, way):
        step = 1 - 2 * way
        if kind == 0:
            src, dst, device = x_sent.at[way], x_got.at[way], (tx + step, ty, me)
        else:
            half = pl.ds((kind - 1) * LANES, LANES)
            src = p_ref.at[:, pl.ds((rows - 8) * (1 - way), 8), half]
            dst = p_ref.at[:, pl.ds(rows + 8 * (1 - way), 8), half]
            device = (tx, ty + step, me)
        return pltpu.make_async_remote_copy(
            src_ref=src, dst_ref=dst, send_sem=sems[0].at[kind, way],
            recv_sem=sems[1].at[kind, way], device_id=device, device_id_type=MESH,
        )

    def start(kind):
        axis = min(kind, 1)
        for way, there in enumerate((has_next[axis], has_prior[axis])):
            pl.when(there)(lambda way=way: copy(kind, way).start())

    def wait(kind):
        axis = min(kind, 1)
        for way in range(2):
            to, source = (has_next[axis], has_prior[axis])[:: 1 - 2 * way]
            pl.when(to)(lambda way=way: copy(kind, way).wait_send())
            pl.when(source)(lambda way=way: copy(kind, way).wait_recv())

    def turn(tile, shift):
        return pltpu.roll(tile, shift % LANES, 1) if shift % LANES else tile

    start(1)

    def pack(q, carry):
        east = west = jnp.zeros((8, LANES), jnp.float32)
        for j in range(2):
            for t in range(8):
                slot = 8 * (8 * j + t)
                tile = p_ref[2 * q + j, 8 * t : 8 * t + 8, :LANES]
                mask = (lane >= slot) & (lane < slot + wide)
                east = jnp.where(mask, turn(tile, slot + wide), east)
                west = jnp.where(mask, turn(tile, slot), west)
        x_sent[0, q] = east
        x_sent[1, q] = west
        return carry

    lax.fori_loop(0, pairs, pack, 0, unroll=3)
    start(0)

    @pl.when(jnp.logical_not(has_prior[0]))
    def _():
        x_got[0] = jnp.zeros(x_got.shape[1:], jnp.float32)

    @pl.when(jnp.logical_not(has_next[0]))
    def _():
        x_got[1] = jnp.zeros(x_got.shape[1:], jnp.float32)

    edge = jnp.zeros((p_ref.shape[0], 8, 2 * LANES), jnp.float32)

    @pl.when(jnp.logical_not(has_prior[1]))
    def _():
        p_ref[:, rows + 8 : rows + 16, :] = edge

    @pl.when(jnp.logical_not(has_next[1]))
    def _():
        p_ref[:, rows : rows + 8, :] = edge

    wait(0)

    def unpack(q, carry):
        low, high = x_got[0, q], x_got[1, q]
        for j in range(2):
            for t in range(8):
                slot = 8 * (8 * j + t)
                tile = jnp.where(lane >= LANES - wide, turn(low, -slot - wide), 0.0)
                tile = jnp.where(lane < wide, turn(high, -slot), tile)
                p_ref[2 * q + j, 8 * t : 8 * t + 8, LANES:] = tile
        return carry

    lax.fori_loop(0, pairs, unpack, 0, unroll=3)
    start(2)
    wait(1)
    wait(2)


def levels_kernel(local, parts, col_rows, n_tx, n_ty, cv_ref, tracer_ref, coef_ref, wet_ref,
                  out_ref, window_ref, p_ref, x_sent, x_got, turned, block, side,
                  rim_send, rim_recv, send_sem, recv_sem):
    tiles = (col_rows + 8) // 8
    coefs = [p_ref.at[local + c] for c in range(3)]
    me = lax.axis_index("gz")
    tx, ty = lax.axis_index("tx"), lax.axis_index("ty")
    peers = [lax.rem(me + d, parts) for d in range(1, parts)]
    lane = lax.broadcasted_iota(jnp.int32, (8, LANES), 1)
    around = [(lax.rem(tx + d, n_tx), ty, me) for d in (1, n_tx - 1)]
    around += [(tx, lax.rem(ty + d, n_ty), me) for d in (1, n_ty - 1)]
    greet([(tx, ty, peer) for peer in peers] + around)
    exchange_rims(
        n_tx, n_ty, tracer_ref, coef_ref, wet_ref, p_ref, x_sent, x_got, (rim_send, rim_recv)
    )

    def chunk(q, carry):
        def level(j, carry):
            l = 5 * q + j
            k = (me * local + l).astype(jnp.float32)
            wet = jnp.where(k < p_ref[local + 3], 1.0, 0.0)
            a = wet * p_ref[l]
            a = substeps(a, wet, *(c[...] * cv_ref[i, me * local + l] for i, c in enumerate(coefs)))
            a = pltpu.roll(a, OFF, 0)
            for part in range(parts):
                for t in range(tiles):
                    row = part * col_rows + 8 * t
                    block[part, q, tiles * j + t] = a[row : row + 8, :LANES]
            side[j] = a[:, LANES:]
            return carry

        lax.fori_loop(0, 5, level, 0)
        for part in range(parts):
            acc = jnp.zeros((8, LANES), jnp.float32)
            for j in range(5):
                for t in range(tiles):
                    slot = 8 * (tiles * j + t)
                    row = part * col_rows + 8 * t
                    tile = pltpu.roll(side[j, row : row + 8, :], slot + NSUB, 1)
                    acc = jnp.where((lane >= slot) & (lane < slot + 2 * NSUB), tile, acc)
            block[part, q, 5 * tiles] = acc
        for peer in peers:
            pltpu.make_async_remote_copy(
                src_ref=block.at[peer, q], dst_ref=out_ref.at[me, q],
                send_sem=send_sem.at[peer, q], recv_sem=recv_sem.at[me, q],
                device_id=(tx, ty, peer), device_id_type=MESH,
            ).start()
        out_ref[me, q] = block[me, q]
        return carry

    chunks = local // 5
    lax.fori_loop(0, chunks, chunk, 0)
    own = pl.ds(pl.multiple_of(me * col_rows, 8), col_rows + 8)
    for c in range(4):
        turned[...] = pltpu.roll(p_ref[local + c], OFF, 0)
        window_ref[c] = turned[own, :]

    def finish(q, carry):
        for peer in peers:
            pltpu.make_async_remote_copy(
                src_ref=block.at[peer, q], dst_ref=out_ref.at[peer, q],
                send_sem=send_sem.at[peer, q], recv_sem=recv_sem.at[peer, q],
                device_id=(tx, ty, peer), device_id_type=MESH,
            ).wait()
        return carry

    lax.fori_loop(0, chunks, finish, 0)


def split(x):
    high = x.astype(jnp.bfloat16)
    return high, (x - high.astype(jnp.float32)).astype(jnp.bfloat16)


def columns_kernel(local, parts, col_rows, n_tx, n_ty, cv_ref, inv_ref, c_ref, m_ref, in_ref,
                   out_ref, sum_ref, main, side, after, field_ref, got_ref, whole_flux, flux_ref,
                   gates, part_flux, tile_flux, *sems):
    levels = local * parts
    me = lax.axis_index("gz")
    tx, ty = lax.axis_index("tx"), lax.axis_index("ty")
    tile, count = tx * n_ty + ty, n_tx * n_ty
    peers = [lax.rem(me + d, parts) for d in range(1, parts)]
    others = [lax.rem(tile + d, count) for d in range(1, count)]
    place = lambda peer: (tx, ty, peer)
    owner = lambda other: (lax.div(other, n_ty), lax.rem(other, n_ty), me)
    gate_rows = lambda at: pl.ds(pl.multiple_of(at * G_DEV, G_DEV), G_DEV)
    run = 8 * local
    span = lambda half, at: pl.ds(pl.multiple_of((half * parts + at) * run, 8), run)
    greet([place(p) for p in peers] + [owner(o) for o in others])

    def copies(kind, own, peer):
        if kind == 2:
            return send(flux_ref.at[peer], part_flux.at[own], sems[4:6], peer, own, place(peer))
        if kind == 3:
            return send(gates.at[gate_rows(peer)], tile_flux.at[own], sems[6:8], peer, own,
                        owner(peer))
        return send(field_ref.at[span(kind, peer)], got_ref.at[span(kind, own)],
                    sems[2 * kind : 2 * kind + 2], peer, own, place(peer))

    tall = col_rows + 8
    tiles = tall // 8
    lane = lax.broadcasted_iota(jnp.int32, (8, LANES), 1)
    rim = (lane < NSUB) | (lane >= LANES - NSUB)

    def unpack(q, carry):
        for part in range(parts):
            packed = in_ref[part, q, 5 * tiles]
            for j in range(5):
                for t in range(tiles):
                    shift = LANES - NSUB - 8 * (tiles * j + t)
                    row = pl.multiple_of((part * local + 5 * q + j) * tall + 8 * t, 8)
                    side[pl.ds(row, 8), :] = jnp.where(rim, pltpu.roll(packed, shift, 1), 0.0)
                    main[pl.ds(row, 8), :] = in_ref[part, q, tiles * j + t]
        return carry

    lax.fori_loop(0, local // 5, unpack, 0)
    inv_high, inv_low = split(inv_ref[...])
    padded = inv_high.shape[0]
    inv_both = jnp.concatenate([inv_high, inv_low], axis=0)
    inv_high = inv_high[:levels]
    ids = lax.broadcasted_iota(jnp.int32, (levels, 2 * LANES), 0).astype(jnp.float32)

    def solve(field, bounds):
        high, low = split(field)
        dot = lambda a, b: jnp.dot(a, b, preferred_element_type=jnp.float32)
        both = dot(inv_both, high)
        out = both[:levels] + (both[padded : padded + levels] + dot(inv_high, low))
        return jnp.where(ids < bounds, out, 0.0)

    for r in range(1, tall - 1):
        at = pl.ds(r, levels, stride=tall)
        field = jnp.concatenate([main[at, :], side[at, :]], axis=1)
        field = solve(field, c_ref[3, r : r + 1, :])
        main[at, :] = field[:, :LANES]
        side[at, :] = field[:, LANES:]

    def group(q, carry):
        for j in range(4):
            k = 4 * q + j
            at = pl.ds(pl.multiple_of(k * tall, 8), tall)
            wet = jnp.where(k.astype(jnp.float32) < c_ref[3], 1.0, 0.0)
            a = jnp.concatenate([main[at, :], side[at, :]], axis=1)
            a = substeps(a, wet, *(c_ref[i] * cv_ref[i, k] for i in range(3)))
            after[at, :] = a[:, :LANES]
        return carry

    lax.fori_loop(0, levels // 4, group, 0)
    pair = lambda ref, r: jnp.concatenate(
        [ref[pl.ds(OFF + r + i, levels, stride=tall), :] for i in range(2)], axis=1
    )
    slot = lambda r: pl.ds((r // 8) * levels * 8 + r % 8, levels, stride=8)
    for r in range(0, col_rows, 2):
        bounds = [c_ref[3, OFF + r + i : OFF + r + i + 1, :LANES] for i in range(2)]
        field = solve(pair(after, r), jnp.concatenate(bounds, axis=1))
        for i in range(2):
            field_ref[slot(r + i), :] = field[:, i * LANES : (i + 1) * LANES]
        if r == 6:
            for peer in peers:
                copies(0, me, peer).start()
    flux = jnp.zeros((whole_flux.shape[0], levels), jnp.float32)
    for r in range(0, col_rows, 2):
        second = jnp.concatenate([field_ref[slot(r + i), :] for i in range(2)], axis=1)
        cells = split(m_ref[:, r * LANES : (r + 2) * LANES])
        total = split(second + pair(main, r))
        for one, two in ((0, 0), (0, 1), (1, 0)):
            flux += lax.dot_general(
                cells[one], total[two], (((1,), (1,)), ((), ())),
                preferred_element_type=jnp.float32,
            )
    whole_flux[...] = jnp.zeros(whole_flux.shape, jnp.float32)
    whole_flux[:, :levels] = flux
    for part in range(parts):
        shift = (LANES - part * local) % LANES
        shifted = whole_flux[...]
        flux_ref[part] = pltpu.roll(shifted, shift, 1) if shift else shifted
    for kind in (2, 1):
        for peer in peers:
            copies(kind, me, peer).start()
    part_flux[me] = flux_ref[me]
    for peer in peers:
        copies(2, peer, peer).wait()
    gates[...] = jnp.sum(part_flux[...], axis=0)
    for other in others:
        copies(3, tile, other).start()
    tile_flux[tile] = gates[gate_rows(tile)]
    for half in range(2):
        got_ref[span(half, me), :] = field_ref[span(half, me), :]
        for peer in peers:
            copies(half, peer, peer).wait()

    def place_level(l, carry):
        for part in range(parts):
            for half in range(2):
                row = pl.multiple_of((half * parts + part) * run + 8 * l, 8)
                start = part * col_rows + 8 * half
                out_ref[l, start : start + 8, :] = got_ref[pl.ds(row, 8), :]
        return carry

    lax.fori_loop(0, local, place_level, 0)
    for other in others:
        copies(3, other, other).wait()
    sum_ref[...] = jnp.sum(tile_flux[...], axis=0)


def per_device(tracer_in, coef_h, coef_v, wet_levels, column_inv, sec_cell, sec_gate, sec_weight):
    depth_count = lax.axis_size("gz")
    depth_index = lax.axis_index("gz")
    tiles = lax.axis_size(("tx", "ty"))
    local_levels, rows, width = tracer_in.shape
    levels = local_levels * depth_count
    col_rows = rows // depth_count
    tall = col_rows + 8
    chunks = local_levels // 5
    row_start = depth_index * col_rows

    gate_ids = jnp.arange(G_DEV * tiles, dtype=jnp.int32)
    gate_hot = jnp.where(gate_ids[:, None] == sec_gate[None, :], sec_weight[None, :], 0.0)
    cells = row_start * width + jnp.arange(col_rows * width, dtype=jnp.int32)
    cell_hot = (sec_cell[:, None] == cells[None, :]).astype(jnp.float32)
    gate_cells = jnp.dot(gate_hot, cell_hot, precision=HI)

    channels = local_levels + 4 + (local_levels + 4) % 2
    blocks = (depth_count, chunks, 5 * tall // 8 + 1, 8, LANES)
    dma = pltpu.SemaphoreType.DMA
    got, window = pl.pallas_call(
        lambda *refs: levels_kernel(
            local_levels, depth_count, col_rows, lax.axis_size("tx"), lax.axis_size("ty"), *refs
        ),
        out_shape=(
            jax.ShapeDtypeStruct(blocks, jnp.float32),
            jax.ShapeDtypeStruct((4, tall, 2 * LANES), jnp.float32),
        ),
        in_specs=[SMEM, VMEM, VMEM, VMEM],
        out_specs=(VMEM, VMEM),
        scratch_shapes=[
            pltpu.VMEM((channels, rows + 16, 2 * LANES), jnp.float32),
            pltpu.VMEM((2, channels // 2, 8, LANES), jnp.float32),
            pltpu.VMEM((2, channels // 2, 8, LANES), jnp.float32),
            pltpu.VMEM((rows + 16, 2 * LANES), jnp.float32),
            pltpu.VMEM(blocks, jnp.float32),
            pltpu.VMEM((5, rows + 16, LANES), jnp.float32),
            dma((3, 2)),
            dma((3, 2)),
            dma((depth_count, chunks)),
            dma((depth_count, chunks)),
        ],
        compiler_params=remote(0),
    )(coef_v, tracer_in, coef_h, wet_levels)

    gates = G_DEV * tiles
    out, flux = pl.pallas_call(
        lambda *refs: columns_kernel(
            local_levels, depth_count, col_rows, lax.axis_size("tx"), lax.axis_size("ty"), *refs
        ),
        out_shape=(
            jax.ShapeDtypeStruct((local_levels, rows, width), jnp.float32),
            jax.ShapeDtypeStruct((G_DEV, LANES), jnp.float32),
        ),
        in_specs=[SMEM, VMEM, VMEM, VMEM, VMEM],
        out_specs=(VMEM, VMEM),
        scratch_shapes=[pltpu.VMEM((levels * tall, LANES), jnp.float32)] * 3
        + [pltpu.VMEM((levels * col_rows, LANES), jnp.float32)] * 2
        + [
            pltpu.VMEM((gates, LANES), jnp.float32),
            pltpu.VMEM((depth_count, gates, LANES), jnp.float32),
            pltpu.VMEM((gates, LANES), jnp.float32),
            pltpu.VMEM((depth_count, gates, LANES), jnp.float32),
            pltpu.VMEM((tiles, G_DEV, LANES), jnp.float32),
        ]
        + [dma((depth_count,))] * 6
        + [dma((tiles,))] * 2,
        compiler_params=remote(1),
    )(coef_v, jnp.pad(column_inv.T, ((0, -levels % 16), (0, 0))), window, gate_cells, got)
    flux = flux[:, :local_levels]
    return (out, flux)


def solution(mesh):
    in_specs = (
        P("gz", "ty", "tx"),
        P(None, "ty", "tx"),
        P(),
        P("ty", "tx"),
        P(),
        P(("tx", "ty")),
        P(("tx", "ty")),
        P(("tx", "ty")),
    )
    out_specs = (P("gz", "ty", "tx"), P(("tx", "ty"), "gz"))
    return jax.shard_map(
        per_device, mesh=mesh, in_specs=in_specs, out_specs=out_specs, check_vma=False
    )
```
